256 devices in a mesh: blk: 128 (over z, x, y_lo, core), rep: 2 (over y_hi).
Axes of the slice: x: 4, y: 4 (y_hi: 2, y_lo: 2; y = y_hi * 2 + y_lo), z: 8, core: 2. Of those that a mesh axis runs over, the one named last changes fastest.
Arguments:
- audio_embed: bfloat16 [65536, 512], P(('rep', 'blk')), parts along dimension 0, may hold values from -1.2 to 1.2
- text_embed: bfloat16 [65536, 512], P(('rep', 'blk')), parts along dimension 0, may hold values from -1.2 to 1.2
- audio_head: bfloat16 [512, 512], replicated, may hold values from -0.25 to 0.25
- text_head: bfloat16 [512, 512], replicated, may hold values from -0.25 to 0.25
- audio_lse: bfloat16 [65536], P(('rep', 'blk')), parts along dimension 0, as said below
- text_lse: bfloat16 [65536], P(('rep', 'blk')), parts along dimension 0, as said below
Outputs:
- audio_input_grad: bfloat16 [65536, 512], P(('rep', 'blk')), parts along dimension 0
- text_input_grad: bfloat16 [65536, 512], P(('rep', 'blk')), parts along dimension 0
- audio_head_grad: float32 [1024, 512], P('rep'), parts along dimension 0
- text_head_grad: float32 [1024, 512], P('rep'), parts along dimension 0
The draws below stay inside these ranges and needn't reach their ends.
There are 2 independent parts, one for each index of `rep`. The reference program is written for one: setup_inputs(seed, part) draws one part's arguments, and reference() takes and returns one part's arrays. A program takes and returns all parts, laid end to end along the dimension named above; an argument that names none is the same for every part. Nothing has to cross between parts.
Inputs may be any that keep to these rules, and one draw needn't show every extreme that they name: Each entry of audio_lse lies between log(8192) - 1.5 and log(8192) + 1.0. Each entry of text_lse lies between log(8192) - 1.5 and log(8192) + 1.0.
All inputs are finite; a program needn't handle non-finite values.
Results may differ from the reference program's by a relative error of at most 0.015.
Values may be sent and summed in bfloat16 or wider, within the bound.
No kernel may reach another device: no remote copies, remote signals or barrier semaphores. Data moves between devices by JAX's collectives and lax.ppermute only.
A program may use at most 64 MiB of HBM per device.

```python
import jax
import jax.numpy as jnp
from jax import lax

EMB = 512
PROJ = 512
ROWS_DEV = 256
WIN = 32
TOKENS = 32768
N_BLK = 128


def embed_rows(key):
    column = jnp.exp(jax.random.uniform(jax.random.fold_in(key, 4), (EMB,), jnp.float32, 0.0, 1.3862944))
    common = jax.random.truncated_normal(jax.random.fold_in(key, 1), -4.0, 4.0, (EMB,), jnp.float32)
    noise = jax.random.truncated_normal(jax.random.fold_in(key, 2), -4.0, 4.0, (TOKENS, EMB), jnp.float32)
    return (0.0215 * column[None, :] * (0.15 * common[None, :] + noise)).astype(jnp.bfloat16)


def lse_rows(key):
    base = jnp.log(jnp.float32(WIN * ROWS_DEV))
    return (base + jax.random.uniform(jax.random.fold_in(key, 2), (TOKENS,), jnp.float32, -1.5, 1.0)).astype(jnp.bfloat16)


def draw_audio_embed(key, part):
    key = jax.random.fold_in(key, 11)
    return embed_rows(key)


def draw_text_embed(key, part):
    key = jax.random.fold_in(key, 12)
    return embed_rows(key)


def draw_audio_lse(key, part):
    key = jax.random.fold_in(key, 13)
    return lse_rows(key)


def draw_text_lse(key, part):
    key = jax.random.fold_in(key, 14)
    return lse_rows(key)


def normal_values(rng, shape, width, limit, held_as=jnp.bfloat16):
    return jnp.clip(width * jax.random.normal(rng, shape, jnp.float32), -limit, limit).astype(held_as)


def setup_inputs(seed: int = 0, part: int = 0) -> dict:
    arg_keys = jax.random.split(jax.random.key(seed), 7)
    part_splits = jax.random.split(jax.random.fold_in(arg_keys[6], part), 7)
    audio_embed = draw_audio_embed(jax.random.fold_in(jax.random.fold_in(arg_keys[6], part), 71), part)
    text_embed = draw_text_embed(jax.random.fold_in(jax.random.fold_in(arg_keys[6], part), 71), part)
    audio_head = normal_values(arg_keys[2], (EMB, PROJ), EMB ** -0.5, 0.25)
    text_head = normal_values(arg_keys[3], (EMB, PROJ), EMB ** -0.5, 0.25)
    audio_lse = draw_audio_lse(jax.random.fold_in(jax.random.fold_in(arg_keys[6], part), 71), part)
    text_lse = draw_text_lse(jax.random.fold_in(jax.random.fold_in(arg_keys[6], part), 71), part)
    return {"audio_embed": audio_embed, "text_embed": text_embed, "audio_head": audio_head, "text_head": text_head, "audio_lse": audio_lse, "text_lse": text_lse}


logit_scale = 14.2857143

def unit_rows(embed, head):
    projected = jnp.dot(embed, head, preferred_element_type=jnp.float32)
    norm_rows = jnp.sqrt(lax.optimization_barrier(jnp.sum(projected * projected, axis=1, keepdims=True)) + 1e-06)
    return (projected / norm_rows, norm_rows)

def head_backward(embed, head, unit, norm_rows, grad, batch_rows):
    dproj = ((grad - unit * lax.optimization_barrier(jnp.sum(unit * grad, axis=1, keepdims=True))) / norm_rows).astype(jnp.bfloat16)
    input_grad = lax.dot_general(dproj, head, (((1,), (1,)), ((), ())), preferred_element_type=jnp.float32).astype(jnp.bfloat16)
    head_grad = lax.dot_general(embed, dproj, (((0,), (0,)), ((), ())), preferred_element_type=jnp.float32) / batch_rows
    return (input_grad, head_grad)

def reference(audio_embed, text_embed, audio_head, text_head, audio_lse, text_lse):
    batch_rows = audio_embed.shape[0]
    row_count = batch_rows // N_BLK
    window_rows = WIN * row_count
    audio_unit, audio_norm = unit_rows(audio_embed, audio_head)
    text_unit, text_norm = unit_rows(text_embed, text_head)
    audio_z = audio_unit.astype(jnp.bfloat16)
    text_z = text_unit.astype(jnp.bfloat16)
    text_wide = jnp.concatenate([text_z, text_z[:window_rows]], axis=0)
    lse_wide = jnp.concatenate([text_lse, text_lse[:window_rows]], axis=0).astype(jnp.float32)
    audio_lse_f = audio_lse.astype(jnp.float32)
    diagonal = jnp.concatenate([jnp.eye(row_count, dtype=jnp.float32), jnp.zeros((row_count, window_rows - row_count), jnp.float32)], axis=1)

    def one_block(state, position):
        offset = (position * row_count).astype(jnp.int32)
        audio_rows = lax.dynamic_slice_in_dim(audio_z, offset, row_count, 0)
        audio_rows_lse = lax.dynamic_slice_in_dim(audio_lse_f, offset, row_count, 0)
        text_rows = lax.dynamic_slice_in_dim(text_wide, offset, window_rows, 0)
        text_rows_lse = lax.dynamic_slice_in_dim(lse_wide, offset, window_rows, 0)
        scores = logit_scale * lax.dot_general(audio_rows, text_rows, (((1,), (1,)), ((), ())), preferred_element_type=jnp.float32)
        weights = (0.5 * (jnp.exp(scores - audio_rows_lse[:, None]) + jnp.exp(scores - text_rows_lse[None, :])) - diagonal).astype(jnp.bfloat16)
        audio_part = logit_scale * jnp.dot(weights, text_rows, preferred_element_type=jnp.float32)
        text_part = logit_scale * lax.dot_general(weights, audio_rows, (((0,), (0,)), ((), ())), preferred_element_type=jnp.float32)
        current = lax.dynamic_slice_in_dim(state, offset, window_rows, 0)
        state = lax.dynamic_update_slice_in_dim(state, current + text_part, offset, 0)
        return (state, audio_part)
    start_state = jnp.zeros((batch_rows + window_rows, text_z.shape[1]), jnp.float32)
    state, audio_parts = lax.scan(one_block, start_state, jnp.arange(N_BLK, dtype=jnp.int32))
    audio_grad = audio_parts.reshape(batch_rows, -1)
    text_grad = state[:batch_rows] + jnp.concatenate([state[batch_rows:], jnp.zeros((batch_rows - window_rows, text_z.shape[1]), jnp.float32)], axis=0)
    audio_input_grad, audio_head_grad = head_backward(audio_embed, audio_head, audio_unit, audio_norm, audio_grad, batch_rows)
    text_input_grad, text_head_grad = head_backward(text_embed, text_head, text_unit, text_norm, text_grad, batch_rows)
    return (audio_input_grad, text_input_grad, audio_head_grad, text_head_grad)
```

```python
import functools

import jax
import jax.numpy as jnp
from jax import lax
from jax.experimental import pallas as pl
from jax.experimental.pallas import tpu as pltpu
from jax.sharding import Mesh, PartitionSpec as P

logit_scale = 14.2857143
log2_e = 1.4426950408889634
PAD = 16

BF = jnp.bfloat16
F32 = jnp.float32
XY = ("x", "yl")


def shift(value, axis, steps):
    count = lax.axis_size(axis)
    return lax.ppermute(value, axis, [(i, (i + steps) % count) for i in range(count)])


def exchange(value, axis):
    return lax.all_to_all(value, axis, split_axis=0, concat_axis=0, tiled=True)


def dot_nn(a, b):
    return jnp.dot(a, b, preferred_element_type=F32)


def dot_nt(a, b):
    return lax.dot_general(a, b, (((1,), (1,)), ((), ())), preferred_element_type=F32)


def dot_tn(a, b):
    return lax.dot_general(a, b, (((0,), (0,)), ((), ())), preferred_element_type=F32)


def tiles_kernel(inv_rows, sel_ref, *refs):
    audio = refs[:5]
    text = refs[5:13]
    ha_ref, ht_ref = refs[13:15]
    da_ref, dt_ref, head_ref = refs[15:18]
    za, zat, zt, ua, ut, na, nt, ea, eb, ga, gt = refs[18:]
    rows, width = za.shape[1], za.shape[2]

    for i in range(5):
        p = dot_nn(audio[i][:rows, :], ha_ref[...])
        inv = lax.rsqrt(jnp.sum(p * p, axis=1, keepdims=True) + 1e-06)
        u = p * inv
        z = u.astype(BF)
        ua[i] = u
        za[i] = z
        zat[i] = z.T
        na[i] = jnp.broadcast_to(inv, na.shape[1:])
        lse = audio[i][rows : rows + PAD, :rows].astype(F32)[0:1, :]
        half = 0.5 * jnp.exp(-lse)
        ea[i] = jnp.broadcast_to(half, (ea.shape[2], rows)).T
    for j in range(4):
        for plane in range(2):
            block = text[4 * plane + j]
            cols = slice(plane * rows, (plane + 1) * rows)
            p = dot_nt(ht_ref[...], block[:rows, :])
            inv = lax.rsqrt(jnp.sum(p * p, axis=0, keepdims=True) + 1e-06)
            u = p * inv
            ut[j, :, cols] = u
            zt[j, :, cols] = u.astype(BF)
            nt[j, :, cols] = jnp.broadcast_to(inv, (8, rows))
            lse = block[rows : rows + PAD, :rows].astype(F32)[0:1, :]
            eb[j, :, cols] = jnp.broadcast_to(0.5 * jnp.exp(-lse), (8, rows))

    ga[...] = jnp.zeros_like(ga)
    row_id = lax.broadcasted_iota(jnp.int32, (rows, 2 * rows), 0)
    col_id = lax.broadcasted_iota(jnp.int32, (rows, 2 * rows), 1)
    eye = (row_id == col_id).astype(F32)

    def chunk(j, carry):
        columns = zt[j]
        col_scale = eb[j, 0:1, :]
        own = sel_ref[j]
        acc = None
        for r in range(4):
            i = own if r == 0 else r + 1
            s = dot_nn(za[i], columns)
            e = jnp.exp2(s * (logit_scale * log2_e))
            row_scale = ea[i]
            scale = jnp.concatenate([row_scale] * (2 * rows // row_scale.shape[1]), axis=1)
            w = e * (scale + col_scale)
            if r == 0:
                w = w - eye * jnp.where(j == 0, 1.0, 0.0)
            w = w.astype(BF)
            ga[i] += dot_nt(w, columns)
            part = dot_nn(zat[i], w)
            acc = part if acc is None else acc + part
        gt[j] = acc
        return carry

    lax.fori_loop(0, 4, chunk, 0)

    head = None
    for i in range(5):
        g = ga[i]
        u = ua[i]
        along = jnp.sum(u * g, axis=1, keepdims=True)
        d = ((g - u * along) * (na[i][:, 0:1] * logit_scale)).astype(BF)
        da_ref[i] = d
        part = dot_tn(audio[i][:rows, :], d)
        head = part if head is None else head + part
    head_ref[0] = (head * inv_rows).astype(BF)
    head = None
    for j in range(4):
        g = gt[j]
        u = ut[j]
        along = jnp.sum(u * g, axis=0, keepdims=True)
        d = ((g - u * along) * (nt[j, 0:1, :] * logit_scale)).astype(BF)
        for plane in range(2):
            part_d = d[:, plane * rows : (plane + 1) * rows]
            dt_ref[2 * j + plane] = part_d
            part = dot_nn(part_d, text[4 * plane + j][:rows, :])
            head = part if head is None else head + part
    head_ref[1] = (head * inv_rows).T.astype(BF)


def tiles(sel, audio, text, audio_head, text_head_t, batch_rows):
    rows, width = audio[0].shape[0] - PAD, audio[0].shape[1]
    lanes = min(128, rows)
    vmem = pl.BlockSpec(memory_space=pltpu.VMEM)
    return pl.pallas_call(
        functools.partial(tiles_kernel, 1.0 / batch_rows),
        out_shape=(
            jax.ShapeDtypeStruct((5, rows, width), BF),
            jax.ShapeDtypeStruct((8, width, rows), BF),
            jax.ShapeDtypeStruct((2, width, width), BF),
        ),
        in_specs=[pl.BlockSpec(memory_space=pltpu.SMEM)] + [vmem] * 15,
        out_specs=(vmem, vmem, vmem),
        scratch_shapes=[
            pltpu.VMEM((5, rows, width), BF),
            pltpu.VMEM((5, width, rows), BF),
            pltpu.VMEM((4, width, 2 * rows), BF),
            pltpu.VMEM((5, rows, width), F32),
            pltpu.VMEM((4, width, 2 * rows), F32),
            pltpu.VMEM((5, rows, lanes), F32),
            pltpu.VMEM((4, 8, 2 * rows), F32),
            pltpu.VMEM((5, rows, lanes), F32),
            pltpu.VMEM((4, 8, 2 * rows), F32),
            pltpu.VMEM((5, rows, width), F32),
            pltpu.VMEM((4, width, 2 * rows), F32),
        ],
        compiler_params=pltpu.CompilerParams(vmem_limit_bytes=48 * 1024 * 1024),
        cost_estimate=pl.CostEstimate(
            flops=12_000_000_000, bytes_accessed=9_000_000, transcendentals=2_100_000
        ),
    )(sel, *audio, *text, audio_head, text_head_t)


def packed(embed, lse):
    extra = jnp.pad(lse[None, :], ((0, PAD - 1), (0, embed.shape[1] - lse.shape[0])))
    return jnp.concatenate([embed, extra], axis=0)


def summed(parts):
    return jnp.sum(parts.astype(F32), axis=0)


def head_total(head):
    core = lax.axis_index("c")
    width = head.shape[1]
    keep = lax.dynamic_index_in_dim(head, core, 0, keepdims=False)
    send = lax.dynamic_index_in_dim(head, 1 - core, 0, keepdims=False)
    mine = (keep.astype(F32) + shift(send, "c", 1).astype(F32)).astype(BF)
    part = summed(exchange(mine, XY).reshape(8, width // 8, width)).astype(BF)
    part = summed(exchange(part, "z").reshape(8, width // 64, width)).astype(BF)
    part = exchange(jnp.broadcast_to(part[None], (8,) + part.shape).reshape(width // 8, width), "z")
    part = exchange(jnp.broadcast_to(part[None], (8,) + part.shape).reshape(width, width), XY)
    other = shift(part, "c", 1)
    first = jnp.where(core == 0, part, other).astype(F32)
    second = jnp.where(core == 0, other, part).astype(F32)
    return first, second


def local(audio_embed, text_embed, audio_head, text_head, audio_lse, text_lse):
    rows = audio_embed.shape[0]
    blocks = lax.axis_size(("z", "x", "yl", "c"))
    x = lax.axis_index("x")
    yl = lax.axis_index("yl")
    core = lax.axis_index("c")

    a_own = packed(audio_embed, audio_lse)
    t_own = packed(text_embed, text_lse)
    t_next = shift(t_own, "z", -1)
    a_prev = shift(a_own, "z", 1)
    t_y = shift(t_own, "yl", 1)
    t_next, a_prev, t_y = lax.optimization_barrier((t_next, a_prev, t_y))
    t_next_y = shift(t_next, "yl", 1)
    a_x = [shift(jnp.where(x + s < 4, a_own, a_prev), "x", s) for s in (1, 2, 3)]
    here = [t_own, t_y]
    here += [shift(v, "c", 1) for v in here]
    ahead = [t_next, t_next_y]
    ahead += [shift(v, "c", 1) for v in ahead]

    behind = [jnp.int32(0), (yl == 1).astype(jnp.int32), (core == 1).astype(jnp.int32), (yl == 1).astype(jnp.int32)]
    da, dt, head = tiles(
        jnp.stack(behind), [a_own, a_prev] + a_x, here + ahead, audio_head, text_head.T, rows * blocks
    )

    audio_total, text_total = head_total(head)

    dt_mine, dt_send = dt[:4], dt[4:]
    dt_sum = (dt_mine.astype(F32) + shift(dt_send, "c", 1).astype(F32)).astype(BF)
    dt_pair = dt_sum[:2].astype(F32) + shift(dt_sum[2:], "yl", 1).astype(F32)
    dt_full = dt_pair[0] + shift(dt_pair[1].astype(BF), "z", 1).astype(F32)
    text_input = lax.dot_general(
        dt_full.astype(BF), text_head, (((0,), (1,)), ((), ())), preferred_element_type=F32
    ).astype(BF)

    back = [shift(da[1 + s], "x", -s).astype(F32) for s in (1, 2, 3)]
    here_sum, behind_sum = da[0].astype(F32), da[1].astype(F32)
    for s in (1, 2, 3):
        wrapped = x + s >= 4
        here_sum = here_sum + jnp.where(wrapped, 0.0, back[s - 1])
        behind_sum = behind_sum + jnp.where(wrapped, back[s - 1], 0.0)
    da_full = here_sum + shift(behind_sum.astype(BF), "z", -1).astype(F32)
    audio_input = dot_nt(da_full.astype(BF), audio_head).astype(BF)
    return audio_input, text_input, audio_total, text_total


def solution(mesh):
    sizes = (8, 4, 2, 2, mesh.shape["rep"])
    grid = Mesh(mesh.devices.reshape(sizes), ("z", "x", "yl", "c", "rep"))
    every = ("rep", "z", "x", "yl", "c")
    return jax.shard_map(
        local,
        mesh=grid,
        in_specs=(P(every, None), P(every, None), P(), P(), P(every), P(every)),
        out_specs=(P(every, None), P(every, None), P("rep", None), P("rep", None)),
        check_vma=False,
    )
```

```python
import functools

import jax
import jax.numpy as jnp
from jax import lax
from jax.experimental import pallas as pl
from jax.experimental.pallas import tpu as pltpu
from jax.sharding import Mesh, PartitionSpec as P

logit_scale = 14.2857143
log2_e = 1.4426950408889634
PAD = 16

BF = jnp.bfloat16
F32 = jnp.float32
XY = ("x", "yl")


def shift(value, axis, steps):
    count = lax.axis_size(axis)
    return lax.ppermute(value, axis, [(i, (i + steps) % count) for i in range(count)])


def exchange(value, axis):
    return lax.all_to_all(value, axis, split_axis=0, concat_axis=0, tiled=True)


def dot_nn(a, b):
    return jnp.dot(a, b, preferred_element_type=F32)


def dot_nt(a, b):
    return lax.dot_general(a, b, (((1,), (1,)), ((), ())), preferred_element_type=F32)


def dot_tn(a, b):
    return lax.dot_general(a, b, (((0,), (0,)), ((), ())), preferred_element_type=F32)


def tiles_kernel(inv_rows, where_ref, *refs):
    audio_x, audio_prev = refs[:2]
    text = refs[2:10]
    ha_ref, ht_ref = refs[10:12]
    dx_ref, dp_ref, mine_ref, send_ref, keep_head, send_head = refs[12:18]
    za, zat, zt, ua, ut, na, nt, ea, eb, ga, gt = refs[18:]
    rows, width = za.shape[1], za.shape[2]
    audio = [audio_x.at[i] for i in range(4)] + [audio_prev]

    for i in range(5):
        p = dot_nn(audio[i][:rows, :], ha_ref[...])
        inv = lax.rsqrt(jnp.sum(p * p, axis=1, keepdims=True) + 1e-06)
        u = p * inv
        z = u.astype(BF)
        ua[i] = u
        za[i] = z
        zat[i] = z.T
        na[i] = jnp.broadcast_to(inv, na.shape[1:])
        lse = audio[i][rows : rows + PAD, :rows].astype(F32)[0:1, :]
        half = 0.5 * jnp.exp(-lse)
        ea[i] = jnp.broadcast_to(half, (ea.shape[2], rows)).T
    for j in range(4):
        for plane in range(2):
            block = text[4 * plane + j]
            cols = slice(plane * rows, (plane + 1) * rows)
            p = dot_nt(ht_ref[...], block[:rows, :])
            inv = lax.rsqrt(jnp.sum(p * p, axis=0, keepdims=True) + 1e-06)
            u = p * inv
            ut[j, :, cols] = u
            zt[j, :, cols] = u.astype(BF)
            nt[j, :, cols] = jnp.broadcast_to(inv, (8, rows))
            lse = block[rows : rows + PAD, :rows].astype(F32)[0:1, :]
            eb[j, :, cols] = jnp.broadcast_to(0.5 * jnp.exp(-lse), (8, rows))

    ga[...] = jnp.zeros_like(ga)
    row_id = lax.broadcasted_iota(jnp.int32, (rows, 2 * rows), 0)
    col_id = lax.broadcasted_iota(jnp.int32, (rows, 2 * rows), 1)
    eye = (row_id == col_id).astype(F32)
    place = where_ref[4]

    def chunk(j, carry):
        columns = zt[j]
        col_scale = eb[j, 0:1, :]
        acc = None
        for r in range(4):
            i = where_ref[j] if r == 0 else lax.rem(place + r, 4)
            s = dot_nn(za[i], columns)
            e = jnp.exp2(s * (logit_scale * log2_e))
            row_scale = ea[i]
            scale = jnp.concatenate([row_scale] * (2 * rows // row_scale.shape[1]), axis=1)
            w = e * (scale + col_scale)
            if r == 0:
                w = w - eye * jnp.where(j == 0, 1.0, 0.0)
            w = w.astype(BF)
            ga[i] += dot_nt(w, columns)
            part = dot_nn(zat[i], w)
            acc = part if acc is None else acc + part
        gt[j] = acc
        return carry

    lax.fori_loop(0, 4, chunk, 0)

    head_a = None
    for i in range(5):
        g = ga[i]
        u = ua[i]
        along = jnp.sum(u * g, axis=1, keepdims=True)
        d = ((g - u * along) * (na[i][:, 0:1] * logit_scale)).astype(BF)
        if i < 4:
            dx_ref[i] = d
        else:
            dp_ref[...] = d
        part = dot_tn(audio[i][:rows, :], d)
        head_a = part if head_a is None else head_a + part
    head_a = (head_a * inv_rows).astype(BF)
    head_t = None
    for j in range(4):
        g = gt[j]
        u = ut[j]
        along = jnp.sum(u * g, axis=0, keepdims=True)
        d = ((g - u * along) * (nt[j, 0:1, :] * logit_scale)).astype(BF)
        out = mine_ref if j < 2 else send_ref
        for plane in range(2):
            part_d = d[:, plane * rows : (plane + 1) * rows]
            out[2 * (j % 2) + plane] = part_d
            part = dot_nn(part_d, text[4 * plane + j][:rows, :])
            head_t = part if head_t is None else head_t + part
    head_t = (head_t * inv_rows).T.astype(BF)
    core = where_ref[5]

    @pl.when(core == 0)
    def _():
        keep_head[...] = head_a
        send_head[...] = head_t

    @pl.when(core == 1)
    def _():
        keep_head[...] = head_t
        send_head[...] = head_a


def tiles(where, audio_x, audio_prev, text, audio_head, text_head_t, batch_rows):
    rows, width = audio_prev.shape[0] - PAD, audio_prev.shape[1]
    lanes = min(128, rows)
    vmem = pl.BlockSpec(memory_space=pltpu.VMEM)
    return pl.pallas_call(
        functools.partial(tiles_kernel, 1.0 / batch_rows),
        out_shape=(
            jax.ShapeDtypeStruct((4, rows, width), BF),
            jax.ShapeDtypeStruct((rows, width), BF),
            jax.ShapeDtypeStruct((4, width, rows), BF),
            jax.ShapeDtypeStruct((4, width, rows), BF),
            jax.ShapeDtypeStruct((width, width), BF),
            jax.ShapeDtypeStruct((width, width), BF),
        ),
        in_specs=[pl.BlockSpec(memory_space=pltpu.SMEM)] + [vmem] * 12,
        out_specs=(vmem,) * 6,
        scratch_shapes=[
            pltpu.VMEM((5, rows, width), BF),
            pltpu.VMEM((5, width, rows), BF),
            pltpu.VMEM((4, width, 2 * rows), BF),
            pltpu.VMEM((5, rows, width), F32),
            pltpu.VMEM((4, width, 2 * rows), F32),
            pltpu.VMEM((5, rows, lanes), F32),
            pltpu.VMEM((4, 8, 2 * rows), F32),
            pltpu.VMEM((5, rows, lanes), F32),
            pltpu.VMEM((4, 8, 2 * rows), F32),
            pltpu.VMEM((5, rows, width), F32),
            pltpu.VMEM((4, width, 2 * rows), F32),
        ],
        compiler_params=pltpu.CompilerParams(vmem_limit_bytes=36 * 1024 * 1024),
        cost_estimate=pl.CostEstimate(
            flops=12_000_000_000, bytes_accessed=9_000_000, transcendentals=2_100_000
        ),
    )(where, audio_x, audio_prev, *text, audio_head, text_head_t)


def packed(embed, lse):
    extra = jnp.pad(lse[None, :], ((0, PAD - 1), (0, embed.shape[1] - lse.shape[0])))
    return jnp.concatenate([embed, extra], axis=0)


def summed(parts):
    return jnp.sum(parts.astype(F32), axis=0)


def repeated(part, count):
    wide = jnp.broadcast_to(part[None], (count,) + part.shape)
    return wide.reshape(count * part.shape[0], part.shape[1])


def head_total(keep, send, other_work):
    width = keep.shape[0]
    mine = (keep.astype(F32) + shift(send, "c", 1).astype(F32)).astype(BF)
    part = summed(exchange(mine, XY).reshape(8, width // 8, width)).astype(BF)
    near = [shift(part, "z", s).astype(F32) for s in (1, -1, -2)]
    part = (part.astype(F32) + near[0] + near[1] + near[2]).astype(BF)
    part = (part.astype(F32) + shift(part, "z", 4).astype(F32)).astype(BF)
    part = exchange(repeated(part, 8), XY)
    part, *other_work = lax.optimization_barrier((part, *other_work))
    other = shift(part, "c", 1)
    core = lax.axis_index("c")
    first = jnp.where(core == 0, part, other).astype(F32)
    second = jnp.where(core == 0, other, part).astype(F32)
    return first, second, *other_work


def local(audio_embed, text_embed, audio_head, text_head, audio_lse, text_lse):
    rows = audio_embed.shape[0]
    blocks = lax.axis_size(("z", "x", "yl", "c"))
    x = lax.axis_index("x")
    yl = lax.axis_index("yl")
    core = lax.axis_index("c")

    a_own = packed(audio_embed, audio_lse)
    t_own = packed(text_embed, text_lse)
    a_prev = shift(a_own, "z", 1)
    t_next = shift(t_own, "z", -1)
    t_y = shift(t_own, "yl", 1)
    t_next, a_prev, t_y = lax.optimization_barrier((t_next, a_prev, t_y))
    for_x = jnp.concatenate([jnp.where(x <= d, a_own, a_prev) for d in range(4)], axis=0)
    audio_x = exchange(for_x, "x").reshape((4,) + a_own.shape)
    t_next_y = shift(t_next, "yl", 1)
    here = [t_own, t_y]
    here += [shift(v, "c", 1) for v in here]
    ahead = [t_next, t_next_y]
    ahead += [shift(v, "c", 1) for v in ahead]

    high_y, high_c = yl == 1, core == 1
    where = [x, jnp.where(high_y, 4, x), jnp.where(high_c, 4, x), jnp.where(high_y, 4, x), x, core]
    dx, dp, dt_mine, dt_send, keep, send = tiles(
        jnp.stack(where), audio_x, a_prev, here + ahead, audio_head, text_head.T, rows * blocks
    )

    dt_sum = (dt_mine.astype(F32) + shift(dt_send, "c", 1).astype(F32)).astype(BF)
    dt_pair = dt_sum[:2].astype(F32) + shift(dt_sum[2:], "yl", 1).astype(F32)
    dt_full = dt_pair[0] + shift(dt_pair[1].astype(BF), "z", 1).astype(F32)
    text_input = lax.dot_general(
        dt_full.astype(BF), text_head, (((0,), (1,)), ((), ())), preferred_element_type=F32
    ).astype(BF)

    back = exchange(dx.reshape(4 * rows, -1), "x").reshape(dx.shape).astype(F32)
    ahead_x = (jnp.arange(4) >= x)[:, None, None]
    here_sum = jnp.sum(jnp.where(ahead_x, back, 0.0), axis=0)
    behind_sum = dp.astype(F32) + jnp.sum(jnp.where(ahead_x, 0.0, back), axis=0)
    da_full = here_sum + shift(behind_sum.astype(BF), "z", -1).astype(F32)
    audio_input = dot_nt(da_full.astype(BF), audio_head).astype(BF)

    audio_total, text_total, audio_input, text_input = head_total(keep, send, (audio_input, text_input))
    return audio_input, text_input, audio_total, text_total


def solution(mesh):
    sizes = (8, 4, 2, 2, mesh.shape["rep"])
    grid = Mesh(mesh.devices.reshape(sizes), ("z", "x", "yl", "c", "rep"))
    every = ("rep", "z", "x", "yl", "c")
    return jax.shard_map(
        local,
        mesh=grid,
        in_specs=(P(every, None), P(every, None), P(), P(), P(every), P(every)),
        out_specs=(P(every, None), P(every, None), P("rep", None), P("rep", None)),
        check_vma=False,
    )
```

```python
import functools

import jax
import jax.numpy as jnp
from jax import lax
from jax.experimental import pallas as pl
from jax.experimental.pallas import tpu as pltpu
from jax.sharding import Mesh, PartitionSpec as P

logit_scale = 14.2857143
log2_e = 1.4426950408889634
PAD = 16

BF = jnp.bfloat16
F32 = jnp.float32
XY = ("x", "yl")


def shift(value, axis, steps):
    count = lax.axis_size(axis)
    return lax.ppermute(value, axis, [(i, (i + steps) % count) for i in range(count)])


def exchange(value, axis):
    return lax.all_to_all(value, axis, split_axis=0, concat_axis=0, tiled=True)


def dot_nn(a, b):
    return jnp.dot(a, b, preferred_element_type=F32)


def dot_nt(a, b):
    return lax.dot_general(a, b, (((1,), (1,)), ((), ())), preferred_element_type=F32)


def tiles_kernel(inv_rows, where_ref, *refs):
    audio_hbm = refs[:5]
    text_hbm = refs[5:13]
    ha_hbm, ht_hbm = refs[13:15]
    da_hbm = refs[15:20]
    mine_hbm, send_hbm, keep_hbm, give_hbm = refs[20:24]
    (ae, al, te, tl, ha, ht, za, zat, zt, ua, ut, na, nt, ea, eb, ga, gt) = refs[24:41]
    (da, dt, keep, give, in_sem, out_sem) = refs[41:]
    width = ha.shape[0]
    rows = ae.shape[0] // 5
    core = where_ref[4]

    def span(first, count=1):
        return slice(first * rows, (first + count) * rows)

    def fetch(block, values, lse, at):
        return [
            (block.at[0:rows, :], values.at[span(at), :]),
            (block.at[rows : rows + PAD, :], lse.at[at]),
        ]

    copies = [(ha_hbm, ha), (ht_hbm, ht)]
    copies += fetch(audio_hbm[0], ae, al, 0)
    for j in range(4):
        for plane in range(2):
            copies += fetch(text_hbm[4 * plane + j], te, tl, 2 * j + plane)
    for i in range(1, 5):
        copies += fetch(audio_hbm[i], ae, al, i)
    copies = [pltpu.make_async_copy(s, d, in_sem.at[i]) for i, (s, d) in enumerate(copies)]
    for c in copies:
        c.start()
    for c in copies[:2]:
        c.wait()
    ha[...] = ha[...].T
    ht[...] = ht[...].T

    def project(head, embeds, cols, u_ref, z_ref, n_ref):
        p = dot_nt(head[...], embeds[cols, :])
        inv = lax.rsqrt(jnp.sum(p * p, axis=0, keepdims=True) + 1e-06)
        u = p * inv
        z = u.astype(BF)
        u_ref[:, cols] = u
        z_ref[:, cols] = z
        n_ref[:, cols] = jnp.broadcast_to(inv, (8, u.shape[1]))
        return z

    def half_exp(lse):
        return 0.5 * jnp.exp(-lse[:, :rows].astype(F32)[0:1, :])

    def audio_block(i):
        z = project(ha, ae, span(i), ua, zat, na)
        za[span(i), :] = z.T
        ea[span(i), :] = jnp.broadcast_to(half_exp(al[i]), (ea.shape[1], rows)).T

    def text_chunk(j):
        project(ht, te, span(2 * j, 2), ut, zt, nt)
        for b in (2 * j, 2 * j + 1):
            eb[:, span(b)] = jnp.broadcast_to(half_exp(tl[b]), (8, rows))

    row_id = lax.broadcasted_iota(jnp.int32, (rows, rows), 0)
    col_id = lax.broadcasted_iota(jnp.int32, (rows, rows), 1)
    eye = (row_id == col_id).astype(F32)

    def tile(j):
        cols = span(2 * j, 2)
        at = pl.ds(pl.multiple_of(where_ref[j] * rows, rows), 4 * rows) if j else span(0, 4)
        z = zt[:, cols]
        e = jnp.exp2(dot_nn(za[at, :], z) * (logit_scale * log2_e))
        row_scale = ea[at, :]
        scale = jnp.concatenate([row_scale] * (2 * rows // row_scale.shape[1]), axis=1)
        w = e * (scale + eb[0:1, cols])
        if j == 0:
            corner = jnp.concatenate([w[:rows, :rows] - eye, w[:rows, rows:]], axis=1)
            w = jnp.concatenate([corner, w[rows:]], axis=0)
        w = w.astype(BF)
        if j == 0:
            ga[:, at] = dot_nt(z, w)
            ga[:, span(4)] = jnp.zeros((width, rows), F32)
        else:
            ga[:, at] += dot_nt(z, w)
        gt[:, cols] = dot_nn(zat[:, at], w)

    for c in copies[2:4]:
        c.wait()
    audio_block(0)
    for c in copies[4:20]:
        c.wait()
    for j in range(4):
        text_chunk(j)
    for c in copies[20:]:
        c.wait()
    for i in range(1, 5):
        audio_block(i)
    for j in range(4):
        tile(j)

    def finish(g_ref, u_ref, n_ref, d_ref, cols):
        g = g_ref[:, cols]
        u = u_ref[:, cols]
        along = jnp.sum(u * g, axis=0, keepdims=True)
        d_ref[:, cols] = ((g - u * along) * (n_ref[0:1, cols] * logit_scale)).astype(BF)

    for j in range(4):
        finish(gt, ut, nt, dt, span(2 * j, 2))
    for i in range(5):
        finish(ga, ua, na, da, span(i))
    outs = [(dt.at[:, span(b)], (mine_hbm if b < 4 else send_hbm).at[b % 4]) for b in range(8)]
    outs += [(da.at[:, span(i)], da_hbm[i]) for i in range(5)]
    outs = [pltpu.make_async_copy(s, d, out_sem.at[i]) for i, (s, d) in enumerate(outs)]
    for c in outs:
        c.start()
    head_t = (dot_nn(dt[...], te[...]) * inv_rows).astype(BF).T
    head_a = (dot_nn(da[...], ae[...]) * inv_rows).astype(BF).T

    @pl.when(core == 0)
    def _():
        keep[...] = head_a
        give[...] = head_t

    @pl.when(core == 1)
    def _():
        keep[...] = head_t
        give[...] = head_a

    last = [(give, give_hbm), (keep, keep_hbm)]
    last = [pltpu.make_async_copy(s, d, out_sem.at[13 + i]) for i, (s, d) in enumerate(last)]
    for c in last:
        c.start()
    for c in outs + last:
        c.wait()


def tiles(where, audio, text, audio_head, text_head, batch_rows):
    rows, width = audio[0].shape[0] - PAD, audio[0].shape[1]
    lanes = min(128, rows)
    anywhere = pl.BlockSpec(memory_space=pl.ANY)
    vmem = pltpu.VMEM
    shape = jax.ShapeDtypeStruct
    return pl.pallas_call(
        functools.partial(tiles_kernel, 1.0 / batch_rows),
        out_shape=(shape((width, rows), BF),) * 5
        + (
            shape((4, width, rows), BF),
            shape((4, width, rows), BF),
            shape((width, width), BF),
            shape((width, width), BF),
        ),
        in_specs=[pl.BlockSpec(memory_space=pltpu.SMEM)] + [anywhere] * 15,
        out_specs=(anywhere,) * 9,
        scratch_shapes=[
            vmem((5 * rows, width), BF),
            vmem((5, PAD, width), BF),
            vmem((8 * rows, width), BF),
            vmem((8, PAD, width), BF),
            vmem((width, width), BF),
            vmem((width, width), BF),
            vmem((5 * rows, width), BF),
            vmem((width, 5 * rows), BF),
            vmem((width, 8 * rows), BF),
            vmem((width, 5 * rows), F32),
            vmem((width, 8 * rows), F32),
            vmem((8, 5 * rows), F32),
            vmem((8, 8 * rows), F32),
            vmem((5 * rows, lanes), F32),
            vmem((8, 8 * rows), F32),
            vmem((width, 5 * rows), F32),
            vmem((width, 8 * rows), F32),
            vmem((width, 5 * rows), BF),
            vmem((width, 8 * rows), BF),
            vmem((width, width), BF),
            vmem((width, width), BF),
            pltpu.SemaphoreType.DMA((28,)),
            pltpu.SemaphoreType.DMA((15,)),
        ],
        compiler_params=pltpu.CompilerParams(vmem_limit_bytes=60 * 1024 * 1024),
        cost_estimate=pl.CostEstimate(
            flops=12_000_000_000, bytes_accessed=9_000_000, transcendentals=2_100_000
        ),
    )(where, *audio, *text, audio_head, text_head)


def packed(embed, lse):
    extra = jnp.pad(lse, ((0, PAD - 1), (0, embed.shape[1] - lse.shape[1])))
    return jnp.concatenate([embed, extra], axis=0)


def diagonal_shift(value, steps):
    count = lax.axis_size("z")
    pairs = [(2 * z + y, 2 * ((z + steps) % count) + 1 - y) for z in range(count) for y in (0, 1)]
    return lax.ppermute(value, ("z", "yl"), pairs)


def summed(parts):
    return jnp.sum(parts.astype(F32), axis=0)


def added(first, *others):
    total = first.astype(F32)
    for other in others:
        total = total + other.astype(F32)
    return total.astype(BF)


def repeated(part, count):
    wide = jnp.broadcast_to(part[None], (count,) + part.shape)
    return wide.reshape(count * part.shape[0], part.shape[1])


def dot_head(dproj_t, head):
    out = lax.dot_general(dproj_t, head, (((0,), (1,)), ((), ())), preferred_element_type=F32)
    return out.astype(BF)


def local(audio_embed, text_embed, audio_head, text_head, audio_lse, text_lse):
    rows, width = audio_embed.shape
    blocks = lax.axis_size(("z", "x", "yl", "c"))
    x = lax.axis_index("x")
    yl = lax.axis_index("yl")
    core = lax.axis_index("c")
    line = ("z", "x")
    together = lax.optimization_barrier

    lse = jnp.stack([audio_lse, text_lse])
    a_own, t_own = together((packed(audio_embed, lse[:1]), packed(text_embed, lse[1:])))
    audio = [a_own] + [shift(a_own, line, s) for s in (1, 2, 3, 4)]
    here = [t_own, shift(t_own, "yl", 1)]
    ahead = [shift(t_own, "z", -1), diagonal_shift(t_own, -1)]
    here += [shift(v, "c", 1) for v in here]
    ahead += [shift(v, "c", 1) for v in ahead]

    behind_y, behind_c = (yl == 1).astype(jnp.int32), (core == 1).astype(jnp.int32)
    where = jnp.stack([jnp.zeros_like(core), behind_y, behind_c, behind_y, core])
    *da, dt_mine, dt_send, keep, give = tiles(
        where, audio, here + ahead, audio_head, text_head, rows * blocks
    )

    head = added(keep, shift(give, "c", 1))
    dt_in = shift(dt_send, "c", 1)
    head = exchange(head, XY)
    dt_sum = added(dt_mine, dt_in)
    back = [shift(da[s], "x", -s) for s in (1, 2, 3)]
    dt_pair = added(dt_sum[:2], shift(dt_sum[2:], "yl", 1))
    here_sum, behind_sum = da[0].astype(F32), da[4].astype(F32)
    for s, part in zip((1, 2, 3), back):
        past = x + s >= 4
        here_sum = here_sum + jnp.where(past, 0.0, part.astype(F32))
        behind_sum = behind_sum + jnp.where(past, part.astype(F32), 0.0)
    dt_ahead = shift(dt_pair[1], "z", 1)
    da_ahead = shift(behind_sum.astype(BF), "z", -1)
    head = summed(head.reshape(8, width // 8, width)).astype(BF)
    head = added(head, *[shift(head, "z", s) for s in (1, -1, -2)])
    far = shift(head, "z", 4)
    head = exchange(repeated(added(head, far), 8), XY)
    audio_input = dot_head(added(here_sum, da_ahead), audio_head)
    text_input = dot_head(added(dt_pair[0], dt_ahead), text_head)
    head, audio_input, text_input = together((head, audio_input, text_input))
    other = shift(head, "c", 1)
    audio_total = jnp.where(core == 0, head, other).astype(F32)
    text_total = jnp.where(core == 0, other, head).astype(F32)
    return audio_input, text_input, audio_total, text_total


def solution(mesh):
    sizes = (8, 4, 2, 2, mesh.shape["rep"])
    grid = Mesh(mesh.devices.reshape(sizes), ("z", "x", "yl", "c", "rep"))
    every = ("rep", "z", "x", "yl", "c")
    return jax.shard_map(
        local,
        mesh=grid,
        in_specs=(P(every, None), P(every, None), P(), P(), P(every), P(every)),
        out_specs=(P(every, None), P(every, None), P("rep", None), P("rep", None)),
        check_vma=False,
    )
```

```python
import functools

import jax
import jax.numpy as jnp
from jax import lax
from jax.experimental import pallas as pl
from jax.experimental.pallas import tpu as pltpu
from jax.sharding import Mesh, PartitionSpec as P

logit_scale = 14.2857143
log2_e = 1.4426950408889634
PAD = 16

BF = jnp.bfloat16
F32 = jnp.float32
XY = ("x", "yl")


def shift(value, axis, steps):
    count = lax.axis_size(axis)
    return lax.ppermute(value, axis, [(i, (i + steps) % count) for i in range(count)])


def exchange(value, axis):
    return lax.all_to_all(value, axis, split_axis=0, concat_axis=0, tiled=True)


def dot_nn(a, b):
    return jnp.dot(a, b, preferred_element_type=F32)


def dot_nt(a, b):
    return lax.dot_general(a, b, (((1,), (1,)), ((), ())), preferred_element_type=F32)


def tiles_kernel(inv_rows, *refs):
    audio_hbm = refs[:5]
    text_hbm = refs[5:13]
    ha_hbm, ht_hbm = refs[13:15]
    da_hbm = refs[15:20]
    mine_hbm, send_hbm, keep_hbm, give_hbm = refs[20:24]
    (ae, al, te, tl, ha, ht, za, zat, zt, ua, ut, na, nt, ea, eb, ga, gt) = refs[24:41]
    (da, dt, keep, give, in_sem, out_sem) = refs[41:]
    width = ha.shape[0]
    rows = ae.shape[0] // 5
    core = lax.axis_index("c")
    high = lax.axis_index("yl")
    first_met = (0, high, core, high)

    def span(first, count=1):
        return slice(first * rows, (first + count) * rows)

    def fetch(block, values, lse, at):
        return [
            (block.at[0:rows, :], values.at[span(at), :]),
            (block.at[rows : rows + PAD, :], lse.at[at]),
        ]

    copies = [(ha_hbm, ha), (ht_hbm, ht)]
    for i in range(5):
        copies += fetch(audio_hbm[i], ae, al, i)
    for j in range(4):
        for plane in range(2):
            copies += fetch(text_hbm[4 * plane + j], te, tl, 2 * j + plane)
    copies = [pltpu.make_async_copy(s, d, in_sem.at[i]) for i, (s, d) in enumerate(copies)]
    for c in copies:
        c.start()
    for c in copies[:2]:
        c.wait()
    ha[...] = ha[...].T
    ht[...] = ht[...].T

    def project(head, embeds, cols, u_ref, z_ref, n_ref):
        p = dot_nt(head[...], embeds[cols, :])
        inv = lax.rsqrt(jnp.sum(p * p, axis=0, keepdims=True) + 1e-06)
        u = p * inv
        z = u.astype(BF)
        u_ref[:, cols] = u
        z_ref[:, cols] = z
        n_ref[:, cols] = jnp.broadcast_to(inv, (8, u.shape[1]))
        return z

    def half_exp(lse):
        return 0.5 * jnp.exp(-lse[:, :rows].astype(F32)[0:1, :])

    def audio_block(i):
        z = project(ha, ae, span(i), ua, zat, na)
        za[span(i), :] = z.T
        ea[span(i), :] = jnp.broadcast_to(half_exp(al[i]), (ea.shape[1], rows)).T

    def text_chunk(j):
        project(ht, te, span(2 * j, 2), ut, zt, nt)
        for b in (2 * j, 2 * j + 1):
            eb[:, span(b)] = jnp.broadcast_to(half_exp(tl[b]), (8, rows))

    row_id = lax.broadcasted_iota(jnp.int32, (rows, rows), 0)
    col_id = lax.broadcasted_iota(jnp.int32, (rows, rows), 1)
    eye = (row_id == col_id).astype(F32)

    def tile(j):
        cols = span(2 * j, 2)
        at = pl.ds(pl.multiple_of(first_met[j] * rows, rows), 4 * rows) if j else span(0, 4)
        z = zt[:, cols]
        e = jnp.exp2(dot_nn(za[at, :], z) * (logit_scale * log2_e))
        row_scale = ea[at, :]
        scale = jnp.concatenate([row_scale] * (2 * rows // row_scale.shape[1]), axis=1)
        w = e * (scale + eb[0:1, cols])
        if j == 0:
            corner = jnp.concatenate([w[:rows, :rows] - eye, w[:rows, rows:]], axis=1)
            w = jnp.concatenate([corner, w[rows:]], axis=0)
        w = w.astype(BF)
        if j == 0:
            ga[:, at] = dot_nt(z, w)
            ga[:, span(4)] = jnp.zeros((width, rows), F32)
        else:
            ga[:, at] += dot_nt(z, w)
        gt[:, cols] = dot_nn(zat[:, at], w)

    def finish(g_ref, u_ref, n_ref, d_ref, cols):
        g = g_ref[:, cols]
        u = u_ref[:, cols]
        along = jnp.sum(u * g, axis=0, keepdims=True)
        d_ref[:, cols] = ((g - u * along) * (n_ref[0:1, cols] * logit_scale)).astype(BF)

    def send(pairs, first):
        sent = [pltpu.make_async_copy(s, d, out_sem.at[first + i]) for i, (s, d) in enumerate(pairs)]
        for c in sent:
            c.start()
        return sent

    for c in copies[2:12]:
        c.wait()
    for i in range(5):
        audio_block(i)
    for c in copies[12:]:
        c.wait()
    outs = []
    for j in range(4):
        text_chunk(j)
    for j in range(4):
        tile(j)
        finish(gt, ut, nt, dt, span(2 * j, 2))
        blocks = (2 * j, 2 * j + 1)
        to = mine_hbm if j < 2 else send_hbm
        outs += send([(dt.at[:, span(b)], to.at[b % 4]) for b in blocks], 2 * j)
    for i in range(5):
        finish(ga, ua, na, da, span(i))
    outs += send([(da.at[:, span(i)], da_hbm[i]) for i in range(5)], 8)
    head_t = (dot_nn(dt[...], te[...]) * inv_rows).astype(BF).T
    head_a = (dot_nn(da[...], ae[...]) * inv_rows).astype(BF).T

    @pl.when(core == 0)
    def _():
        keep[...] = head_a
        give[...] = head_t

    @pl.when(core == 1)
    def _():
        keep[...] = head_t
        give[...] = head_a

    outs += send([(give, give_hbm), (keep, keep_hbm)], 13)
    for c in outs:
        c.wait()


def tiles(audio, text, audio_head, text_head, batch_rows):
    rows, width = audio[0].shape[0] - PAD, audio[0].shape[1]
    lanes = min(128, rows)
    anywhere = pl.BlockSpec(memory_space=pl.ANY)
    vmem = pltpu.VMEM
    shape = jax.ShapeDtypeStruct
    return pl.pallas_call(
        functools.partial(tiles_kernel, 1.0 / batch_rows),
        out_shape=(shape((width, rows), BF),) * 5
        + (
            shape((4, width, rows), BF),
            shape((4, width, rows), BF),
            shape((width, width), BF),
            shape((width, width), BF),
        ),
        in_specs=[anywhere] * 15,
        out_specs=(anywhere,) * 9,
        scratch_shapes=[
            vmem((5 * rows, width), BF),
            vmem((5, PAD, width), BF),
            vmem((8 * rows, width), BF),
            vmem((8, PAD, width), BF),
            vmem((width, width), BF),
            vmem((width, width), BF),
            vmem((5 * rows, width), BF),
            vmem((width, 5 * rows), BF),
            vmem((width, 8 * rows), BF),
            vmem((width, 5 * rows), F32),
            vmem((width, 8 * rows), F32),
            vmem((8, 5 * rows), F32),
            vmem((8, 8 * rows), F32),
            vmem((5 * rows, lanes), F32),
            vmem((8, 8 * rows), F32),
            vmem((width, 5 * rows), F32),
            vmem((width, 8 * rows), F32),
            vmem((width, 5 * rows), BF),
            vmem((width, 8 * rows), BF),
            vmem((width, width), BF),
            vmem((width, width), BF),
            pltpu.SemaphoreType.DMA((28,)),
            pltpu.SemaphoreType.DMA((15,)),
        ],
        compiler_params=pltpu.CompilerParams(vmem_limit_bytes=60 * 1024 * 1024),
        cost_estimate=pl.CostEstimate(
            flops=12_000_000_000, bytes_accessed=9_000_000, transcendentals=2_100_000
        ),
    )(*audio, *text, audio_head, text_head)


def packed(embed, lse):
    extra = jnp.pad(lse, ((0, PAD - 1), (0, embed.shape[1] - lse.shape[1])))
    return jnp.concatenate([embed, extra], axis=0)


def diagonal_shift(value, steps):
    count = lax.axis_size("z")
    pairs = [(2 * z + y, 2 * ((z + steps) % count) + 1 - y) for z in range(count) for y in (0, 1)]
    return lax.ppermute(value, ("z", "yl"), pairs)


def summed(parts):
    return jnp.sum(parts.astype(F32), axis=0)


def added(first, *others):
    total = first.astype(F32)
    for other in others:
        total = total + other.astype(F32)
    return total.astype(BF)


def repeated(part, count):
    wide = jnp.broadcast_to(part[None], (count,) + part.shape)
    return wide.reshape(count * part.shape[0], part.shape[1])


def dot_head(dproj_t, head):
    out = lax.dot_general(dproj_t, head, (((0,), (1,)), ((), ())), preferred_element_type=F32)
    return out.astype(BF)


def local(audio_embed, text_embed, audio_head, text_head, audio_lse, text_lse):
    rows, width = audio_embed.shape
    blocks = lax.axis_size(("z", "x", "yl", "c"))
    x = lax.axis_index("x")
    yl = lax.axis_index("yl")
    core = lax.axis_index("c")
    line = ("z", "x")
    together = lax.optimization_barrier

    lse = jnp.stack([audio_lse, text_lse])
    a_own, t_own = together((packed(audio_embed, lse[:1]), packed(text_embed, lse[1:])))
    a_4 = shift(a_own, line, 4)
    a_1 = shift(a_own, line, 1)
    t_y = shift(t_own, "yl", 1)
    t_next = shift(t_own, "z", -1)
    t_next_y = diagonal_shift(t_own, -1)
    t_c = shift(t_own, "c", 1)
    a_2 = shift(jnp.where(x + 2 < 4, a_own, a_4), "x", 2)
    a_3 = shift(jnp.where(x + 3 < 4, a_own, a_4), "x", 3)
    t_y, t_next, t_next_y, a_2, a_3 = together((t_y, t_next, t_next_y, a_2, a_3))
    audio = [a_own, a_1, a_2, a_3, a_4]
    here = [t_own, t_y, t_c, shift(t_y, "c", 1)]
    ahead = [t_next, t_next_y, shift(t_next, "c", 1), shift(t_next_y, "c", 1)]

    *da, dt_mine, dt_send, keep, give = tiles(
        audio, here + ahead, audio_head, text_head, rows * blocks
    )

    head = added(keep, shift(give, "c", 1))
    dt_in = shift(dt_send, "c", 1)
    head = exchange(head, XY)
    dt_sum = added(dt_mine, dt_in)
    back = [shift(da[s], "x", -s) for s in (1, 2, 3)]
    dt_pair = added(dt_sum[:2], shift(dt_sum[2:], "yl", 1))
    here_sum, behind_sum = da[0].astype(F32), da[4].astype(F32)
    for s, part in zip((1, 2, 3), back):
        past = x + s >= 4
        here_sum = here_sum + jnp.where(past, 0.0, part.astype(F32))
        behind_sum = behind_sum + jnp.where(past, part.astype(F32), 0.0)
    behind_sum = behind_sum.astype(BF)
    dt_ahead = shift(dt_pair[1], "z", 1)
    da_ahead = shift(behind_sum, "z", -1)
    head = summed(head.reshape(8, width // 8, width)).astype(BF)
    head = added(head, *[shift(head, "z", s) for s in (1, -1, -2)])
    far = shift(head, "z", 4)
    head = exchange(repeated(added(head, far), 8), XY)
    audio_input = dot_head(added(here_sum, da_ahead), audio_head)
    text_input = dot_head(added(dt_pair[0], dt_ahead), text_head)
    head, audio_input, text_input = together((head, audio_input, text_input))
    other = shift(head, "c", 1)
    audio_total = jnp.where(core == 0, head, other).astype(F32)
    text_total = jnp.where(core == 0, other, head).astype(F32)
    return audio_input, text_input, audio_total, text_total


def solution(mesh):
    sizes = (8, 4, 2, 2, mesh.shape["rep"])
    grid = Mesh(mesh.devices.reshape(sizes), ("z", "x", "yl", "c", "rep"))
    every = ("rep", "z", "x", "yl", "c")
    return jax.shard_map(
        local,
        mesh=grid,
        in_specs=(P(every, None), P(every, None), P(), P(), P(every), P(every)),
        out_specs=(P(every, None), P(every, None), P("rep", None), P("rep", None)),
        check_vma=False,
    )
```

```python
import functools

import jax
import jax.numpy as jnp
from jax import lax
from jax.experimental import pallas as pl
from jax.experimental.pallas import tpu as pltpu
from jax.sharding import Mesh, PartitionSpec as P

logit_scale = 14.2857143
log2_e = 1.4426950408889634
PAD = 16

BF = jnp.bfloat16
F32 = jnp.float32
XY = ("x", "yl")


def shift(value, axis, steps):
    count = lax.axis_size(axis)
    return lax.ppermute(value, axis, [(i, (i + steps) % count) for i in range(count)])


def exchange(value, axis):
    return lax.all_to_all(value, axis, split_axis=0, concat_axis=0, tiled=True)


def dot_nn(a, b):
    return jnp.dot(a, b, preferred_element_type=F32)


def dot_nt(a, b):
    return lax.dot_general(a, b, (((1,), (1,)), ((), ())), preferred_element_type=F32)


def tiles_kernel(inv_rows, *refs):
    audio_hbm = refs[:5]
    text_hbm = refs[5:13]
    ha_hbm, ht_hbm = refs[13:15]
    da_hbm = refs[15:20]
    mine_hbm, send_hbm, keep, give = refs[20:24]
    (ae, al, te, tl, ha, ht, za, zat, zt, ua, ut, na, nt, ea, eb, ga, gt) = refs[24:41]
    (da, dt, in_sem, out_sem) = refs[41:]
    width = ha.shape[0]
    rows = ae.shape[0] // 5
    core = lax.axis_index("c")
    high = lax.axis_index("yl")
    first_met = (0, high, core, high)

    def span(first, count=1):
        return slice(first * rows, (first + count) * rows)

    def fetch(block, values, lse, at):
        return [
            (block.at[0:rows, :], values.at[span(at), :]),
            (block.at[rows : rows + PAD, :], lse.at[at]),
        ]

    copies = [(ha_hbm, ha), (ht_hbm, ht)]
    for i in range(5):
        copies += fetch(audio_hbm[i], ae, al, i)
    for j in range(4):
        for plane in range(2):
            copies += fetch(text_hbm[4 * plane + j], te, tl, 2 * j + plane)
    copies = [pltpu.make_async_copy(s, d, in_sem.at[i]) for i, (s, d) in enumerate(copies)]
    for c in copies:
        c.start()
    for c in copies[:2]:
        c.wait()
    ha[...] = ha[...].T
    ht[...] = ht[...].T

    def project(head, embeds, cols, u_ref, z_ref, n_ref):
        p = dot_nt(head[...], embeds[cols, :])
        inv = lax.rsqrt(jnp.sum(p * p, axis=0, keepdims=True) + 1e-06)
        u = p * inv
        z = u.astype(BF)
        u_ref[:, cols] = u
        z_ref[:, cols] = z
        n_ref[:, cols] = jnp.broadcast_to(inv, (8, u.shape[1]))
        return z

    def half_exp(lse):
        return 0.5 * jnp.exp(-lse[:, :rows].astype(F32)[0:1, :])

    def audio_block(i):
        z = project(ha, ae, span(i), ua, zat, na)
        za[span(i), :] = z.T
        ea[span(i), :] = jnp.broadcast_to(half_exp(al[i]), (ea.shape[1], rows)).T

    def text_chunk(j):
        project(ht, te, span(2 * j, 2), ut, zt, nt)
        for b in (2 * j, 2 * j + 1):
            eb[:, span(b)] = jnp.broadcast_to(half_exp(tl[b]), (8, rows))

    row_id = lax.broadcasted_iota(jnp.int32, (rows, rows), 0)
    col_id = lax.broadcasted_iota(jnp.int32, (rows, rows), 1)
    eye = (row_id == col_id).astype(F32)

    def tile(j):
        cols = span(2 * j, 2)
        at = pl.ds(pl.multiple_of(first_met[j] * rows, rows), 4 * rows) if j else span(0, 4)
        z = zt[:, cols]
        e = jnp.exp2(dot_nn(za[at, :], z) * (logit_scale * log2_e))
        row_scale = ea[at, :]
        scale = jnp.concatenate([row_scale] * (2 * rows // row_scale.shape[1]), axis=1)
        w = e * (scale + eb[0:1, cols])
        if j == 0:
            corner = jnp.concatenate([w[:rows, :rows] - eye, w[:rows, rows:]], axis=1)
            w = jnp.concatenate([corner, w[rows:]], axis=0)
        w = w.astype(BF)
        if j == 0:
            ga[:, at] = dot_nt(z, w)
            ga[:, span(4)] = jnp.zeros((width, rows), F32)
        else:
            ga[:, at] += dot_nt(z, w)
        gt[:, cols] = dot_nn(zat[:, at], w)

    def finish(g_ref, u_ref, n_ref, d_ref, cols):
        g = g_ref[:, cols]
        u = u_ref[:, cols]
        along = jnp.sum(u * g, axis=0, keepdims=True)
        d_ref[:, cols] = ((g - u * along) * (n_ref[0:1, cols] * logit_scale)).astype(BF)

    def send(pairs, first):
        sent = [pltpu.make_async_copy(s, d, out_sem.at[first + i]) for i, (s, d) in enumerate(pairs)]
        for c in sent:
            c.start()
        return sent

    for c in copies[2:12]:
        c.wait()
    for i in range(5):
        audio_block(i)
    for c in copies[12:]:
        c.wait()
    outs = []
    for j in range(4):
        text_chunk(j)
    for j in range(4):
        tile(j)
        finish(gt, ut, nt, dt, span(2 * j, 2))
        blocks = (2 * j, 2 * j + 1)
        to = mine_hbm if j < 2 else send_hbm
        outs += send([(dt.at[:, span(b)], to.at[b % 4]) for b in blocks], 2 * j)
    for i in range(5):
        finish(ga, ua, na, da, span(i))
    outs += send([(da.at[:, span(i)], da_hbm[i]) for i in range(5)], 8)
    head_t = (dot_nn(dt[...], te[...]) * inv_rows).astype(BF).T
    head_a = (dot_nn(da[...], ae[...]) * inv_rows).astype(BF).T

    @pl.when(core == 0)
    def _():
        keep[...] = head_a
        give[...] = head_t

    @pl.when(core == 1)
    def _():
        keep[...] = head_t
        give[...] = head_a

    for c in outs:
        c.wait()


def tiles(audio, text, audio_head, text_head, batch_rows):
    rows, width = audio[0].shape[0] - PAD, audio[0].shape[1]
    lanes = min(128, rows)
    anywhere = pl.BlockSpec(memory_space=pl.ANY)
    vmem = pltpu.VMEM
    shape = jax.ShapeDtypeStruct
    return pl.pallas_call(
        functools.partial(tiles_kernel, 1.0 / batch_rows),
        out_shape=(shape((width, rows), BF),) * 5
        + (
            shape((4, width, rows), BF),
            shape((4, width, rows), BF),
            shape((width, width), BF),
            shape((width, width), BF),
        ),
        in_specs=[anywhere] * 15,
        out_specs=(anywhere,) * 7 + (pl.BlockSpec(memory_space=pltpu.VMEM),) * 2,
        scratch_shapes=[
            vmem((5 * rows, width), BF),
            vmem((5, PAD, width), BF),
            vmem((8 * rows, width), BF),
            vmem((8, PAD, width), BF),
            vmem((width, width), BF),
            vmem((width, width), BF),
            vmem((5 * rows, width), BF),
            vmem((width, 5 * rows), BF),
            vmem((width, 8 * rows), BF),
            vmem((width, 5 * rows), F32),
            vmem((width, 8 * rows), F32),
            vmem((8, 5 * rows), F32),
            vmem((8, 8 * rows), F32),
            vmem((5 * rows, lanes), F32),
            vmem((8, 8 * rows), F32),
            vmem((width, 5 * rows), F32),
            vmem((width, 8 * rows), F32),
            vmem((width, 5 * rows), BF),
            vmem((width, 8 * rows), BF),
            pltpu.SemaphoreType.DMA((28,)),
            pltpu.SemaphoreType.DMA((13,)),
        ],
        compiler_params=pltpu.CompilerParams(vmem_limit_bytes=48 * 1024 * 1024),
        cost_estimate=pl.CostEstimate(
            flops=12_000_000_000, bytes_accessed=9_000_000, transcendentals=2_100_000
        ),
    )(*audio, *text, audio_head, text_head)


def packed(embed, lse):
    extra = jnp.pad(lse, ((0, PAD - 1), (0, embed.shape[1] - lse.shape[1])))
    return jnp.concatenate([embed, extra], axis=0)


def diagonal_shift(value, steps):
    count = lax.axis_size("z")
    pairs = [(2 * z + y, 2 * ((z + steps) % count) + 1 - y) for z in range(count) for y in (0, 1)]
    return lax.ppermute(value, ("z", "yl"), pairs)


def summed(parts):
    return jnp.sum(parts.astype(F32), axis=0)


def added(first, *others):
    total = first.astype(F32)
    for other in others:
        total = total + other.astype(F32)
    return total.astype(BF)


def repeated(part, count):
    wide = jnp.broadcast_to(part[None], (count,) + part.shape)
    return wide.reshape(count * part.shape[0], part.shape[1])


def dot_head(dproj_t, head):
    out = lax.dot_general(dproj_t, head, (((0,), (1,)), ((), ())), preferred_element_type=F32)
    return out.astype(BF)


def local(audio_embed, text_embed, audio_head, text_head, audio_lse, text_lse):
    rows, width = audio_embed.shape
    blocks = lax.axis_size(("z", "x", "yl", "c"))
    x = lax.axis_index("x")
    yl = lax.axis_index("yl")
    core = lax.axis_index("c")
    line = ("z", "x")
    together = lax.optimization_barrier

    lse = jnp.stack([audio_lse, text_lse])
    a_own, t_own = together((packed(audio_embed, lse[:1]), packed(text_embed, lse[1:])))
    a_4 = shift(a_own, line, 4)
    a_1 = shift(a_own, line, 1)
    t_y = shift(t_own, "yl", 1)
    t_next = shift(t_own, "z", -1)
    t_next_y = diagonal_shift(t_own, -1)
    t_c = shift(t_own, "c", 1)
    a_2 = shift(jnp.where(x + 2 < 4, a_own, a_4), "x", 2)
    a_3 = shift(jnp.where(x + 3 < 4, a_own, a_4), "x", 3)
    t_next_y, a_2, a_3 = together((t_next_y, a_2, a_3))
    audio = [a_own, a_1, a_2, a_3, a_4]
    here = [t_own, t_y, t_c, shift(t_y, "c", 1)]
    ahead = [t_next, t_next_y, shift(t_next, "c", 1), shift(t_next_y, "c", 1)]

    *da, dt_mine, dt_send, keep, give = tiles(
        audio, here + ahead, audio_head, text_head, rows * blocks
    )

    head = added(keep, shift(give, "c", 1))
    dt_in = shift(dt_send, "c", 1)
    head = exchange(head, XY)
    dt_sum = added(dt_mine, dt_in)
    back = [shift(da[s], "x", -s) for s in (1, 2, 3)]
    dt_pair = added(dt_sum[:2], shift(dt_sum[2:], "yl", 1))
    here_sum, behind_sum = da[0].astype(F32), da[4].astype(F32)
    for s, part in zip((1, 2, 3), back):
        past = x + s >= 4
        here_sum = here_sum + jnp.where(past, 0.0, part.astype(F32))
        behind_sum = behind_sum + jnp.where(past, part.astype(F32), 0.0)
    behind_sum = behind_sum.astype(BF)
    dt_ahead = shift(dt_pair[1], "z", 1)
    da_ahead = shift(behind_sum, "z", -1)
    head = summed(head.reshape(8, width // 8, width)).astype(BF)
    head = added(head, *[shift(head, "z", s) for s in (1, -1, -2)])
    far = shift(head, "z", 4)
    head = exchange(repeated(added(head, far), 8), XY)
    audio_input = dot_head(added(here_sum, da_ahead), audio_head)
    text_input = dot_head(added(dt_pair[0], dt_ahead), text_head)
    head, audio_input, text_input = together((head, audio_input, text_input))
    other = shift(head, "c", 1)
    audio_total = jnp.where(core == 0, head, other).astype(F32)
    text_total = jnp.where(core == 0, other, head).astype(F32)
    return audio_input, text_input, audio_total, text_total


def solution(mesh):
    sizes = (8, 4, 2, 2, mesh.shape["rep"])
    grid = Mesh(mesh.devices.reshape(sizes), ("z", "x", "yl", "c", "rep"))
    every = ("rep", "z", "x", "yl", "c")
    return jax.shard_map(
        local,
        mesh=grid,
        in_specs=(P(every, None), P(every, None), P(), P(), P(every), P(every)),
        out_specs=(P(every, None), P(every, None), P("rep", None), P("rep", None)),
        check_vma=False,
    )
```
